32 devices in a mesh: dp: 4 (over y, x), gr: 2 (over core), gc: 4 (over z).
Axes of the slice: x: 2, y: 2, z: 4, core: 2. Of those that a mesh axis runs over, the one named last changes fastest.
Arguments:
- frames: float32 [4, 1500, 768], P('dp', 'gc', 'gr'), may hold values from -6 to 6
- cotangent: float32 [4, 1500, 768], P('dp', 'gc', 'gr'), may hold values from -6 to 6
- w_qkv: float32 [768, 3, 768], P('gr', None, 'gc'), may hold values from -0.21875 to 0.21875
- w_out: float32 [768, 768], P('gc', 'gr'), may hold values from -6 to 6
- w_up: float32 [768, 3072], P('gr', 'gc'), may hold values from -0.21875 to 0.21875
- w_down: float32 [3072, 768], P('gc', 'gr'), may hold values from -0.109375 to 0.109375
- vectors: float32 [6, 768], P(None, 'gr'), may hold values from -0.8 to 1.5, as said below
- first_qkv: float32 [768, 3, 768], P(('gr', 'dp'), None, 'gc'), may hold values from -48 to 48
- second_qkv: float32 [768, 3, 768], P(('gr', 'dp'), None, 'gc'), may hold values from 6 to 24
- first_out: float32 [768, 768], P('gc', ('gr', 'dp')), may hold values from -6 to 6
- second_out: float32 [768, 768], P('gc', ('gr', 'dp')), may hold values from 0.015 to 0.06
- first_up: float32 [768, 3072], P(('gr', 'dp'), 'gc'), may hold values from -24 to 24
- second_up: float32 [768, 3072], P(('gr', 'dp'), 'gc'), may hold values from 1.5 to 6
- first_down: float32 [3072, 768], P('gc', ('gr', 'dp')), may hold values from -32 to 32
- second_down: float32 [3072, 768], P('gc', ('gr', 'dp')), may hold values from 2.16 to 8.64
- first_vec: float32 [6, 768], P(None, 'gr'), may hold values from -80 to 80
- second_vec: float32 [6, 768], P(None, 'gr'), may hold values from 13.5 to 54
Outputs:
- block_out: float32 [4, 1500, 768], P('dp', 'gc', 'gr')
- grad_frames: float32 [4, 1500, 768], P('dp', 'gc', 'gr')
- grad_qkv: float32 [768, 3, 768], P(('gr', 'dp'), None, 'gc')
- first_qkv_new: float32 [768, 3, 768], P(('gr', 'dp'), None, 'gc')
- second_qkv_new: float32 [768, 3, 768], P(('gr', 'dp'), None, 'gc')
- w_qkv_new: float32 [768, 3, 768], P(('gr', 'dp'), None, 'gc')
- grad_out: float32 [768, 768], P('gc', ('gr', 'dp'))
- first_out_new: float32 [768, 768], P('gc', ('gr', 'dp'))
- second_out_new: float32 [768, 768], P('gc', ('gr', 'dp'))
- w_out_new: float32 [768, 768], P('gc', ('gr', 'dp'))
- grad_up: float32 [768, 3072], P(('gr', 'dp'), 'gc')
- first_up_new: float32 [768, 3072], P(('gr', 'dp'), 'gc')
- second_up_new: float32 [768, 3072], P(('gr', 'dp'), 'gc')
- w_up_new: float32 [768, 3072], P(('gr', 'dp'), 'gc')
- grad_down: float32 [3072, 768], P('gc', ('gr', 'dp'))
- first_down_new: float32 [3072, 768], P('gc', ('gr', 'dp'))
- second_down_new: float32 [3072, 768], P('gc', ('gr', 'dp'))
- w_down_new: float32 [3072, 768], P('gc', ('gr', 'dp'))
- grad_vectors: float32 [6, 768], P(None, 'gr')
- first_vec_new: float32 [6, 768], P(None, 'gr')
- second_vec_new: float32 [6, 768], P(None, 'gr')
- vectors_new: float32 [6, 768], P(None, 'gr')
The draws below stay inside these ranges and needn't reach their ends.
Inputs may be any that keep to these rules, and one draw needn't show every extreme that they name: `vectors`: rows 0 and 3 lie in 0.5 to 1.5; the other rows in -0.8 to 0.8.
All inputs are finite; a program needn't handle non-finite values.
Results may differ from the reference program's by a relative error of at most 0.00018.
Values sent between devices are 32-bit elements; how exact they have to be, the bound alone decides.
A program may use at most 128 MiB of HBM per device.

```python
import math
import jax
import jax.numpy as jnp
from jax import lax

D = 768
HEADS = 12
HD = 64
FF = 3072
LEN = 1500
STEP = 10
CLIPS = 4
TOKENS = 6000


def draw_vectors(key, part):
    key = jax.random.fold_in(key, 5)
    gain_key, bias_key = jax.random.split(key)
    gains = jnp.clip(1.0 + 0.2 * jax.random.normal(gain_key, (6, D), jnp.float32), 0.5, 1.5)
    biases = jnp.clip(0.4 * jax.random.normal(bias_key, (6, D), jnp.float32), -0.8, 0.8)
    row_index = jnp.arange(6)[:, None]
    is_gain = (row_index == 0) | (row_index == 3)
    return jnp.where(is_gain, gains, biases)


def steps_of(key, extent, pieces, low, top_value):
    loudness, own = 1.0, jax.random.fold_in(key, 6)
    for dim, shards_of in pieces:
        steps = jnp.exp(jax.random.uniform(jax.random.fold_in(own, dim), (shards_of,), jnp.float32, low / len(pieces), top_value / len(pieces)))
        loudness = loudness * jnp.repeat(steps, extent[dim] // shards_of).reshape([-1 if axis == dim else 1 for axis in range(len(extent))])
    return loudness


def centred(key, dims, scale, most, shards=(), held_as=jnp.bfloat16):
    factor_of = steps_of(key, dims, shards, -0.22, 0.18) if shards else 1.0
    entries = jax.random.normal(key, dims, jnp.float32) * scale * factor_of
    return jnp.minimum(jnp.maximum(entries, -most), most).astype(held_as)


def setup_inputs(seed: int = 0) -> dict:
    splits = jax.random.split(jax.random.key(seed), 18)
    frames = centred(splits[0], (CLIPS, LEN, D), 1.0, 6.0, ((0, 4), (1, 4), (2, 2)), jnp.float32)
    cotangent = centred(splits[1], (CLIPS, LEN, D), 1.0, 6.0, ((0, 4), (1, 4), (2, 2)), jnp.float32)
    w_qkv = centred(splits[2], (D, 3, D), D ** -0.5, 0.21875, ((0, 2), (2, 4)), jnp.float32)
    w_out = centred(splits[3], (D, D), ((LEN / (2.7 * D)) ** 0.5), 6.0, ((0, 4), (1, 2)), jnp.float32)
    w_up = centred(splits[4], (D, FF), D ** -0.5, 0.21875, ((0, 2), (1, 4)), jnp.float32)
    w_down = centred(splits[5], (FF, D), FF ** -0.5, 0.109375, ((0, 4), (1, 2)), jnp.float32)
    vectors = draw_vectors(jax.random.fold_in(splits[17], 71), 0)
    first_qkv = centred(splits[7], (D, 3, D), (0.11 * TOKENS ** 0.5), 48.0, ((0, 8), (2, 4)), jnp.float32)
    second_qkv = jnp.clip(jnp.exp(math.log(24.0) - 1.3862944 * jax.random.uniform(splits[8], (D, 3, D), jnp.float32) ** steps_of(splits[8], (D, 3, D), ((0, 8), (2, 4)), -0.2, 0.2)), 6.0, 24.0)
    first_out = centred(splits[9], (D, D), (0.0055 * TOKENS ** 0.5), 6.0, ((0, 4), (1, 8)), jnp.float32)
    second_out = jnp.clip(jnp.exp(math.log(0.06) - 1.3862944 * jax.random.uniform(splits[10], (D, D), jnp.float32) ** steps_of(splits[10], (D, D), ((0, 4), (1, 8)), -0.2, 0.2)), 0.015, 0.06)
    first_up = centred(splits[11], (D, FF), (0.055 * TOKENS ** 0.5), 24.0, ((0, 8), (1, 4)), jnp.float32)
    second_up = jnp.clip(jnp.exp(math.log(6.0) - 1.3862944 * jax.random.uniform(splits[12], (D, FF), jnp.float32) ** steps_of(splits[12], (D, FF), ((0, 8), (1, 4)), -0.2, 0.2)), 1.5, 6.0)
    first_down = centred(splits[13], (FF, D), (0.066 * TOKENS ** 0.5), 32.0, ((0, 4), (1, 8)), jnp.float32)
    second_down = jnp.clip(jnp.exp(math.log(8.64) - 1.3862944 * jax.random.uniform(splits[14], (FF, D), jnp.float32) ** steps_of(splits[14], (FF, D), ((0, 4), (1, 8)), -0.2, 0.2)), 2.16, 8.64)
    first_vec = centred(splits[15], (6, D), (0.165 * TOKENS ** 0.5), 80.0, ((1, 2),), jnp.float32)
    second_vec = jnp.clip(jnp.exp(math.log(54.0) - 1.3862944 * jax.random.uniform(splits[16], (6, D), jnp.float32) ** steps_of(splits[16], (6, D), ((1, 2),), -0.2, 0.2)), 13.5, 54.0)
    return {"frames": frames, "cotangent": cotangent, "w_qkv": w_qkv, "w_out": w_out, "w_up": w_up, "w_down": w_down, "vectors": vectors, "first_qkv": first_qkv, "second_qkv": second_qkv, "first_out": first_out, "second_out": second_out, "first_up": first_up, "second_up": second_up, "first_down": first_down, "second_down": second_down, "first_vec": first_vec, "second_vec": second_vec}


norm_eps = 1e-05
learn_rate = 0.1
beta_first = 0.9
beta_second = 0.999
adam_epsilon = 1e-08
weight_decay = 0.01
highest = lax.Precision.HIGHEST

def layer_norm(inputs, norm_gain, norm_bias):
    center = inputs - lax.optimization_barrier(jnp.mean(inputs, -1, keepdims=True))
    spread = lax.optimization_barrier(jnp.mean(center * center, -1, keepdims=True))
    return center * lax.rsqrt(spread + norm_eps) * norm_gain + norm_bias

def attend(inputs):
    queries, key_block, value_block = inputs
    scores = jnp.einsum('qhe,khe->hqk', queries, key_block, precision=highest) * HD ** (-0.5)
    weights = jax.nn.softmax(scores, axis=-1)
    return jnp.einsum('hqk,khe->qhe', weights, value_block, precision=highest)

def forward(frames, w_qkv, w_out, w_up, w_down, vectors):
    normed = layer_norm(frames, vectors[0], vectors[1])
    mixed_qkv = jnp.einsum('cld,djn->cljn', normed, w_qkv, precision=highest)
    split_qkv = mixed_qkv.reshape(CLIPS, LEN, 3, HEADS, HD)
    head_out = lax.map(jax.checkpoint(attend), (split_qkv[:, :, 0], split_qkv[:, :, 1], split_qkv[:, :, 2]))
    attended = head_out.reshape(CLIPS, LEN, D)
    middle = frames + jnp.einsum('cln,nd->cld', attended, w_out, precision=highest) + vectors[2]
    normed_two = layer_norm(middle, vectors[3], vectors[4])
    hidden = jnp.einsum('cld,df->clf', normed_two, w_up, precision=highest)
    active = jax.nn.gelu(hidden, approximate=False)
    return middle + jnp.einsum('clf,fd->cld', active, w_down, precision=highest) + vectors[5]

def adamw(weight_old, gradient, first_old, second_old, decay_rate):
    first_new = beta_first * first_old + (1.0 - beta_first) * gradient
    second_new = beta_second * second_old + (1.0 - beta_second) * gradient * gradient
    step_dir = first_new / (1.0 - beta_first ** STEP) / (jnp.sqrt(second_new / (1.0 - beta_second ** STEP)) + adam_epsilon)
    return (first_new, second_new, weight_old - learn_rate * (step_dir + decay_rate * weight_old))

def reference(frames, cotangent, w_qkv, w_out, w_up, w_down, vectors, first_qkv, second_qkv, first_out, second_out, first_up, second_up, first_down, second_down, first_vec, second_vec):
    block_out, pullback = jax.vjp(forward, frames, w_qkv, w_out, w_up, w_down, vectors)
    grad_frames, grad_qkv, grad_out, grad_up, grad_down, grad_vectors = pullback(cotangent)
    first_qkv_new, second_qkv_new, w_qkv_new = adamw(w_qkv, grad_qkv, first_qkv, second_qkv, weight_decay)
    first_out_new, second_out_new, w_out_new = adamw(w_out, grad_out, first_out, second_out, weight_decay)
    first_up_new, second_up_new, w_up_new = adamw(w_up, grad_up, first_up, second_up, weight_decay)
    first_down_new, second_down_new, w_down_new = adamw(w_down, grad_down, first_down, second_down, weight_decay)
    first_vec_new, second_vec_new, vectors_new = adamw(vectors, grad_vectors, first_vec, second_vec, 0.0)
    return (block_out, grad_frames, grad_qkv, first_qkv_new, second_qkv_new, w_qkv_new, grad_out, first_out_new, second_out_new, w_out_new, grad_up, first_up_new, second_up_new, w_up_new, grad_down, first_down_new, second_down_new, w_down_new, grad_vectors, first_vec_new, second_vec_new, vectors_new)
```

```python
import functools

import jax
import jax.numpy as jnp
from jax import lax
from jax.experimental import pallas as pl
from jax.experimental.pallas import tpu as pltpu
from jax.sharding import PartitionSpec as P

HD = 64
STEP = 10


norm_eps = 1e-05
learn_rate = 0.1
beta_first = 0.9
beta_second = 0.999
adam_epsilon = 1e-08
weight_decay = 0.01
high = lax.Precision.HIGH
swap_pairs = ((0, 1), (1, 0))
row_tile = 64
masked = -1e30


def product(spec, left, right):
    return jnp.einsum(spec, left, right, precision=high)


def gather_tokens(rows):
    return lax.all_gather(rows, "gc", axis=0, tiled=True)


def scatter_tokens(partial_value):
    return lax.psum_scatter(partial_value, "gc", scatter_dimension=0, tiled=True)


def other_core(value):
    return lax.ppermute(value, "gr", swap_pairs)


def in_core_order(mine, theirs, axis):
    first = lax.axis_index("gr") == 0
    return jnp.concatenate((jnp.where(first, mine, theirs), jnp.where(first, theirs, mine)), axis)


def own_rows(piece, row_count):
    padded = jnp.pad(piece, ((0, 2 * row_count - piece.shape[0]), (0, 0)))
    core = lax.axis_index("gr")
    mine = lax.dynamic_slice_in_dim(padded, core * row_count, row_count, 0)
    sent = lax.dynamic_slice_in_dim(padded, (1 - core) * row_count, row_count, 0)
    return in_core_order(mine, other_core(sent), 1)


def own_width(rows, frame_count):
    half = rows.shape[1] // 2
    core = lax.axis_index("gr")
    mine = lax.dynamic_slice_in_dim(rows, core * half, half, 1)
    sent = lax.dynamic_slice_in_dim(rows, (1 - core) * half, half, 1)
    return in_core_order(mine, other_core(sent), 0)[:frame_count]


def own_half_sum(partial_value):
    half = partial_value.shape[0] // 2
    core = lax.axis_index("gr")
    mine = lax.dynamic_slice_in_dim(partial_value, core * half, half, 0)
    sent = lax.dynamic_slice_in_dim(partial_value, (1 - core) * half, half, 0)
    return mine + other_core(sent)


def norm_forward(inputs, norm_gain, norm_bias):
    average = jnp.mean(inputs, -1, keepdims=True)
    centred = inputs - average
    row_scale = lax.rsqrt(jnp.mean(centred * centred, -1, keepdims=True) + norm_eps)
    normalized = centred * row_scale
    return (normalized * norm_gain + norm_bias, normalized, row_scale)


def norm_backward(grad_normed, normalized, row_scale, norm_gain):
    grad_unit = grad_normed * norm_gain
    grad_inputs = row_scale * (
        grad_unit
        - jnp.mean(grad_unit, -1, keepdims=True)
        - normalized * jnp.mean(grad_unit * normalized, -1, keepdims=True)
    )
    return (grad_inputs, jnp.sum(grad_normed * normalized, 0), jnp.sum(grad_normed, 0))


def split_parts(value):
    upper = value.astype(jnp.bfloat16)
    return upper, (value - upper.astype(jnp.float32)).astype(jnp.bfloat16)


def left_three(value):
    upper, lower = split_parts(value)
    return jnp.concatenate((upper, upper, lower), -1)


def right_three(value):
    upper, lower = split_parts(value)
    return jnp.concatenate((upper, lower, upper), -1)


def dot_rows(left, right):
    return lax.dot_general(left, right, (((1,), (1,)), ((), ())), preferred_element_type=jnp.float32)


def dot_plain(left, right):
    return jnp.dot(left, right, preferred_element_type=jnp.float32)


def attend_kernel(heads, q_ref, k_ref, vt_ref, mask_ref, out_ref, lse_ref, k_three, vt_two):
    @pl.when(pl.program_id(0) == 0)
    def _():
        for head in range(heads):
            cols = slice(head * HD, (head + 1) * HD)
            k_three[head] = left_three(k_ref[:, cols])
            vt_two[head] = jnp.concatenate(split_parts(vt_ref[cols, :]), 0)

    for head in range(heads):
        cols = slice(head * HD, (head + 1) * HD)
        q_three = right_three(q_ref[:, cols] * HD ** (-0.5))
        scores = dot_rows(k_three[head], q_three) + mask_ref[...]
        top = jnp.max(scores, 0, keepdims=True)
        weights = jnp.exp(scores - top)
        totals = jnp.sum(weights, 0, keepdims=True)
        upper, lower = split_parts(weights)
        both = dot_plain(vt_two[head], upper)
        summed = both[:HD] + both[HD:] + dot_plain(vt_two[head, :HD], lower)
        out_ref[cols, :] = summed / totals
        lse_ref[head : head + 1, :] = top + jnp.log(totals)


def attend_back_kernel(
    heads, q_ref, k_ref, v_ref, kt_ref, mask_ref, lse_ref, delta_ref, do_ref,
    dq_ref, dk_ref, dv_ref, k_three, v_three, kt_two,
):
    @pl.when(pl.program_id(0) == 0)
    def _():
        for head in range(heads):
            cols = slice(head * HD, (head + 1) * HD)
            k_three[head] = left_three(k_ref[:, cols])
            v_three[head] = left_three(v_ref[:, cols])
            kt_two[head] = jnp.concatenate(split_parts(kt_ref[cols, :]), 0)
        dk_ref[...] = jnp.zeros_like(dk_ref)
        dv_ref[...] = jnp.zeros_like(dv_ref)

    for head in range(heads):
        cols = slice(head * HD, (head + 1) * HD)
        q_up, q_low = split_parts(q_ref[:, cols] * HD ** (-0.5))
        do_up, do_low = split_parts(do_ref[:, cols])
        scores = dot_rows(k_three[head], jnp.concatenate((q_up, q_low, q_up), -1)) + mask_ref[...]
        weights = jnp.exp(scores - lse_ref[head : head + 1, :])
        grad_weights = dot_rows(v_three[head], jnp.concatenate((do_up, do_low, do_up), -1))
        grad_scores = weights * (grad_weights - delta_ref[head : head + 1, :])
        w_up, w_low = split_parts(weights)
        both = dot_plain(w_up, jnp.concatenate((do_up, do_low), -1))
        dv_ref[:, cols] += both[:, :HD] + both[:, HD:] + dot_plain(w_low, do_up)
        s_up, s_low = split_parts(grad_scores)
        both = dot_plain(s_up, jnp.concatenate((q_up, q_low), -1))
        dk_ref[:, cols] += both[:, :HD] + both[:, HD:] + dot_plain(s_low, q_up)
        both = dot_plain(kt_two[head], s_up)
        summed = both[:HD] + both[HD:] + dot_plain(kt_two[head, :HD], s_low)
        dq_ref[cols, :] = summed * HD ** (-0.5)


def whole(*dims):
    return pl.BlockSpec(dims, lambda step: (0,) * len(dims))


def query_block(count):
    for size in (256, 128):
        if count % size == 0:
            return size
    return count


def attend_forward(queries, keys_all, values_all, mask):
    count, columns = queries.shape
    key_count, heads = keys_all.shape[0], columns // HD
    block = query_block(count)
    return pl.pallas_call(
        functools.partial(attend_kernel, heads),
        grid=(count // block,),
        in_specs=[
            pl.BlockSpec((block, columns), lambda step: (step, 0)),
            whole(key_count, columns),
            whole(columns, key_count),
            whole(key_count, 1),
        ],
        out_specs=[
            pl.BlockSpec((columns, block), lambda step: (0, step)),
            pl.BlockSpec((heads, block), lambda step: (0, step)),
        ],
        out_shape=[
            jax.ShapeDtypeStruct((columns, count), jnp.float32),
            jax.ShapeDtypeStruct((heads, count), jnp.float32),
        ],
        scratch_shapes=[
            pltpu.VMEM((heads, key_count, 3 * HD), jnp.bfloat16),
            pltpu.VMEM((heads, 2 * HD, key_count), jnp.bfloat16),
        ],
        compiler_params=pltpu.CompilerParams(vmem_limit_bytes=48 * 2**20),
        cost_estimate=pl.CostEstimate(
            flops=12 * count * key_count * columns,
            bytes_accessed=16 * key_count * columns,
            transcendentals=count * key_count * heads,
        ),
    )(queries, keys_all, values_all.T, mask)


def attend_backward(queries, keys_all, values_all, mask, lse, delta, grad_attn):
    count, columns = queries.shape
    key_count, heads = keys_all.shape[0], columns // HD
    block = query_block(count)
    return pl.pallas_call(
        functools.partial(attend_back_kernel, heads),
        grid=(count // block,),
        in_specs=[
            pl.BlockSpec((block, columns), lambda step: (step, 0)),
            whole(key_count, columns),
            whole(key_count, columns),
            whole(columns, key_count),
            whole(key_count, 1),
            pl.BlockSpec((heads, block), lambda step: (0, step)),
            pl.BlockSpec((heads, block), lambda step: (0, step)),
            pl.BlockSpec((block, columns), lambda step: (step, 0)),
        ],
        out_specs=[
            pl.BlockSpec((columns, block), lambda step: (0, step)),
            whole(key_count, columns),
            whole(key_count, columns),
        ],
        out_shape=[
            jax.ShapeDtypeStruct((columns, count), jnp.float32),
            jax.ShapeDtypeStruct((key_count, columns), jnp.float32),
            jax.ShapeDtypeStruct((key_count, columns), jnp.float32),
        ],
        scratch_shapes=[
            pltpu.VMEM((heads, key_count, 3 * HD), jnp.bfloat16),
            pltpu.VMEM((heads, key_count, 3 * HD), jnp.bfloat16),
            pltpu.VMEM((heads, 2 * HD, key_count), jnp.bfloat16),
        ],
        compiler_params=pltpu.CompilerParams(vmem_limit_bytes=48 * 2**20),
        cost_estimate=pl.CostEstimate(
            flops=30 * count * key_count * columns,
            bytes_accessed=24 * key_count * columns,
            transcendentals=count * key_count * heads,
        ),
    )(queries, keys_all, values_all, keys_all.T, mask, lse, delta, grad_attn)


def owned_block(weight_block, dim_index, owned_count):
    return lax.dynamic_slice_in_dim(
        weight_block, lax.axis_index("dp") * owned_count, owned_count, dim_index
    )


def adamw(weight_old, gradient, first_old, second_old, decay_rate):
    first_new = beta_first * first_old + (1.0 - beta_first) * gradient
    second_new = beta_second * second_old + (1.0 - beta_second) * gradient * gradient
    step_dir = (
        first_new
        / (1.0 - beta_first**STEP)
        / (jnp.sqrt(second_new / (1.0 - beta_second**STEP)) + adam_epsilon)
    )
    return (first_new, second_new, weight_old - learn_rate * (step_dir + decay_rate * weight_old))


def local(
    frames,
    cotangent,
    w_qkv,
    w_out,
    w_up,
    w_down,
    vectors,
    first_qkv,
    second_qkv,
    first_out,
    second_out,
    first_up,
    second_up,
    first_down,
    second_down,
    first_vec,
    second_vec,
):
    frame_count, half_width = frames.shape[1:]
    width, columns = 2 * half_width, w_qkv.shape[2]
    local_heads = columns // HD
    core = lax.axis_index("gr")
    row_count = -(-frame_count // (2 * row_tile)) * row_tile
    chips = lax.axis_size("gc")
    count = chips * row_count

    vectors_all = lax.all_gather(vectors, "gr", axis=1, tiled=True)
    rows = own_rows(frames[0], row_count)
    normed, unit_one, scale_one = norm_forward(rows, vectors_all[0], vectors_all[1])
    normed_all = gather_tokens(normed)
    weights_qkv = in_core_order(w_qkv, other_core(w_qkv), 0).reshape(width, 3 * columns)
    weights_out = in_core_order(w_out, other_core(w_out), 1)
    weights_up = in_core_order(w_up, other_core(w_up), 0)
    weights_down = in_core_order(w_down, other_core(w_down), 1)
    grad_rows = own_rows(cotangent[0], row_count)
    grad_all = gather_tokens(grad_rows)

    mixed_qkv = product("td,dn->tn", normed_all, weights_qkv)
    queries = mixed_qkv[:, :columns]
    key_value = mixed_qkv[:, columns:]
    key_value_all = in_core_order(key_value, other_core(key_value), 0)
    keys_all, values_all = key_value_all[:, :columns], key_value_all[:, columns:]
    place = jnp.arange(2 * count)
    real = place // count * row_count + place % row_count < frame_count
    mask = jnp.where(real, 0.0, masked).astype(jnp.float32)[:, None]
    attended_t, lse = attend_forward(queries, keys_all, values_all, mask)

    middle = rows + scatter_tokens(product("nt,nd->td", attended_t, weights_out)) + vectors_all[2]
    normed_two, unit_two, scale_two = norm_forward(middle, vectors_all[3], vectors_all[4])
    normed_two_all = gather_tokens(normed_two)
    grad_active = product("td,fd->tf", grad_all, weights_down)
    hidden = product("td,df->tf", normed_two_all, weights_up)
    cumulative = 0.5 * (1.0 + lax.erf(hidden * 0.5**0.5))
    density = jnp.exp(-0.5 * hidden * hidden) * (0.5 / jnp.pi) ** 0.5
    active = hidden * cumulative
    grad_hidden = grad_active * (cumulative + hidden * density)
    grad_normed_two = scatter_tokens(product("tf,df->td", grad_hidden, weights_up))
    grad_middle_norm, grad_gain_two, grad_bias_two = norm_backward(
        grad_normed_two, unit_two, scale_two, vectors_all[3]
    )
    grad_middle = grad_rows + grad_middle_norm
    grad_middle_all = gather_tokens(grad_middle)

    block_rows = middle + scatter_tokens(product("tf,fd->td", active, weights_down)) + vectors_all[5]
    block_out = own_width(block_rows, frame_count)[None]
    grad_down = own_half_sum(product("tf,td->df", active, grad_all))
    grad_up = own_half_sum(product("td,tf->df", normed_two_all, grad_hidden))
    grad_out = own_half_sum(product("nt,td->dn", attended_t, grad_middle_all))

    grad_attn = product("td,nd->tn", grad_middle_all, weights_out)
    delta = jnp.sum((grad_attn.T * attended_t).reshape(local_heads, HD, count), 1)
    grad_queries_t, grad_keys, grad_values = attend_backward(
        queries, keys_all, values_all, mask, lse, delta, grad_attn
    )
    grad_pairs = jnp.concatenate((grad_keys, grad_values), 1)
    mine = lax.dynamic_slice_in_dim(grad_pairs, core * count, count, 0)
    sent = lax.dynamic_slice_in_dim(grad_pairs, (1 - core) * count, count, 0)
    grad_mixed = jnp.concatenate((grad_queries_t.T, mine + other_core(sent)), 1)
    grad_normed = scatter_tokens(product("tn,dn->td", grad_mixed, weights_qkv))
    grad_qkv = own_half_sum(product("td,tn->dn", normed_all, grad_mixed))
    grad_inputs, grad_gain_one, grad_bias_one = norm_backward(
        grad_normed, unit_one, scale_one, vectors_all[0]
    )
    grad_frames = own_width(grad_middle + grad_inputs, frame_count)[None]

    vector_local = jnp.stack(
        (
            grad_gain_one,
            grad_bias_one,
            jnp.sum(grad_middle, 0),
            grad_gain_two,
            grad_bias_two,
            jnp.sum(grad_rows, 0),
        )
    )
    grad_vectors = lax.psum(vector_local, ("dp", "gr", "gc"))
    grad_vectors = lax.dynamic_slice_in_dim(grad_vectors, core * half_width, half_width, 1)
    grad_down, grad_up, grad_out, grad_qkv = (
        lax.psum_scatter(part, "dp", scatter_dimension=0, tiled=True)
        for part in (grad_down, grad_up, grad_out, grad_qkv)
    )
    grad_down, grad_out = grad_down.T, grad_out.T
    grad_qkv = grad_qkv.reshape(grad_qkv.shape[0], 3, columns)
    first_qkv_new, second_qkv_new, w_qkv_new = adamw(
        owned_block(w_qkv, 0, grad_qkv.shape[0]), grad_qkv, first_qkv, second_qkv, weight_decay
    )
    first_out_new, second_out_new, w_out_new = adamw(
        owned_block(w_out, 1, grad_out.shape[1]), grad_out, first_out, second_out, weight_decay
    )
    first_up_new, second_up_new, w_up_new = adamw(
        owned_block(w_up, 0, grad_up.shape[0]), grad_up, first_up, second_up, weight_decay
    )
    first_down_new, second_down_new, w_down_new = adamw(
        owned_block(w_down, 1, grad_down.shape[1]), grad_down, first_down, second_down, weight_decay
    )
    first_vec_new, second_vec_new, vectors_new = adamw(
        vectors, grad_vectors, first_vec, second_vec, 0.0
    )
    return (
        block_out,
        grad_frames,
        grad_qkv,
        first_qkv_new,
        second_qkv_new,
        w_qkv_new,
        grad_out,
        first_out_new,
        second_out_new,
        w_out_new,
        grad_up,
        first_up_new,
        second_up_new,
        w_up_new,
        grad_down,
        first_down_new,
        second_down_new,
        w_down_new,
        grad_vectors,
        first_vec_new,
        second_vec_new,
        vectors_new,
    )


def solution(mesh):
    return jax.shard_map(
        local,
        mesh=mesh,
        in_specs=(
            P("dp", "gc", "gr"),
            P("dp", "gc", "gr"),
            P("gr", None, "gc"),
            P("gc", "gr"),
            P("gr", "gc"),
            P("gc", "gr"),
            P(None, "gr"),
            P(("gr", "dp"), None, "gc"),
            P(("gr", "dp"), None, "gc"),
            P("gc", ("gr", "dp")),
            P("gc", ("gr", "dp")),
            P(("gr", "dp"), "gc"),
            P(("gr", "dp"), "gc"),
            P("gc", ("gr", "dp")),
            P("gc", ("gr", "dp")),
            P(None, "gr"),
            P(None, "gr"),
        ),
        out_specs=(
            P("dp", "gc", "gr"),
            P("dp", "gc", "gr"),
            P(("gr", "dp"), None, "gc"),
            P(("gr", "dp"), None, "gc"),
            P(("gr", "dp"), None, "gc"),
            P(("gr", "dp"), None, "gc"),
            P("gc", ("gr", "dp")),
            P("gc", ("gr", "dp")),
            P("gc", ("gr", "dp")),
            P("gc", ("gr", "dp")),
            P(("gr", "dp"), "gc"),
            P(("gr", "dp"), "gc"),
            P(("gr", "dp"), "gc"),
            P(("gr", "dp"), "gc"),
            P("gc", ("gr", "dp")),
            P("gc", ("gr", "dp")),
            P("gc", ("gr", "dp")),
            P("gc", ("gr", "dp")),
            P(None, "gr"),
            P(None, "gr"),
            P(None, "gr"),
            P(None, "gr"),
        ),
        check_vma=False,
    )
```
